128 devices in a mesh: leaf: 32 (over z, y, core), rows: 4 (over x).
Axes of the slice: x: 4, y: 4, z: 4, core: 2. Of those that a mesh axis runs over, the one named last changes fastest.
Arguments:
- sigma_top: float32 [8192, 1024], P('leaf'), may hold values from -4 to 40, as said below
- panel_top: float32 [1024, 49152], P(None, 'leaf'), may hold values from -0.125 to 0.125
- diag_top: float32 [49152, 256], P('leaf'), may hold values from -4 to 20, as said below
- panel_mid: float32 [1024, 98304], P(None, ('leaf', 'rows')), may hold values from -0.125 to 0.125
- diag_mid: float32 [98304, 256], P(('leaf', 'rows')), may hold values from -4 to 20, as said below
- pattern_mid: int32 [16, 4], replicated, may hold values from 0 to 23, as said below
- panel_low: float32 [1024, 196608], P(None, ('leaf', 'rows')), may hold values from -0.125 to 0.125
- diag_low: float32 [196608, 256], P(('leaf', 'rows')), may hold values from -4 to 20, as said below
- pattern_low: int32 [32, 4], replicated, may hold values from 0 to 23, as said below
Outputs:
- cross_top: float32 [1024, 49152], P('rows', 'leaf')
- marginal_top: float32 [49152, 256], P(('leaf', 'rows'))
- cross_mid: float32 [1024, 98304], P(None, ('leaf', 'rows'))
- marginal_mid: float32 [98304, 256], P(('leaf', 'rows'))
- cross_low: float32 [1024, 196608], P(None, ('leaf', 'rows'))
- marginal_low: float32 [196608, 256], P(('leaf', 'rows'))
The draws below stay inside these ranges and needn't reach their ends.
Inputs may be any that keep to these rules, and one draw needn't show every extreme that they name: Each block of 1024 rows of sigma_top is symmetric. `diag_top`: each 256 x 256 block is symmetric. `diag_mid`: each block of 256 rows is symmetric. `diag_low`: each block of 256 rows is symmetric. `pattern_mid`: the 4 entries of a row are different; rows 2i and 2i + 1 together name 8 different blocks. `pattern_low`: the 4 entries of a row are different; rows 2i and 2i + 1 together name 8 different blocks.
All inputs are finite; a program needn't handle non-finite values.
Results may differ from the reference program's by a relative error of at most 0.00009.
Values sent between devices are 32-bit elements; how exact they have to be, the bound alone decides.
No kernel may reach another device: no remote copies, remote signals or barrier semaphores. Data moves between devices by JAX's collectives and lax.ppermute only.
A program may use at most 192 MiB of HBM per device.

```python
import math
import jax
import jax.numpy as jnp
from jax import lax

BLOCK = 256
NBLOCK = 24
STRUCT_BLOCKS = 4
ORDER = 6144
STRUCT = 1024
NTOP = 8
NMID = 16
NLOW = 32


def symmetric_blocks(key, block_count, block_side, base_low, base_high, off_scale):
    key_rough, key_levels = jax.random.split(key, 2)
    rough_part = jax.random.normal(key_rough, (block_count, block_side, block_side), jnp.float32)
    mixed_part = (rough_part + jnp.swapaxes(rough_part, 1, 2)) * (off_scale / math.sqrt(2.0 * block_side))
    levels = jnp.exp(jax.random.uniform(key_levels, (block_count, block_side), jnp.float32, math.log(base_low), math.log(base_high)))
    eye_table = jnp.eye(block_side, dtype=jnp.float32)
    whole_set = mixed_part + eye_table[None, :, :] * levels[:, :, None]
    return whole_set


def pattern_rows(key, row_total):
    order_perm = jax.random.permutation(key, NBLOCK).astype(jnp.int32)
    spots = (jnp.arange(row_total * STRUCT_BLOCKS, dtype=jnp.int32) % NBLOCK).reshape(row_total, STRUCT_BLOCKS)
    return order_perm[spots]


def draw_sigma_top(key, part):
    return symmetric_blocks(jax.random.fold_in(key, 11), NTOP, STRUCT, 1.0, 4.0, 0.45).reshape(NTOP * STRUCT, STRUCT)


def draw_diag_top(key, part):
    return symmetric_blocks(jax.random.fold_in(key, 12), NTOP * NBLOCK, BLOCK, 0.5, 2.0, 0.3).reshape(NTOP * ORDER, BLOCK)


def draw_diag_mid(key, part):
    return symmetric_blocks(jax.random.fold_in(key, 13), NMID * NBLOCK, BLOCK, 0.5, 2.0, 0.3).reshape(NMID * ORDER, BLOCK)


def draw_diag_low(key, part):
    return symmetric_blocks(jax.random.fold_in(key, 14), NLOW * NBLOCK, BLOCK, 0.5, 2.0, 0.3).reshape(NLOW * ORDER, BLOCK)


def draw_pattern_mid(key, part):
    return pattern_rows(jax.random.fold_in(key, 15), NMID)


def draw_pattern_low(key, part):
    return pattern_rows(jax.random.fold_in(key, 16), NLOW)


def level_of(stream_key, shape, cuts, low, top_value):
    loudness = 1.0
    for position, parts in cuts:
        heights = jax.random.uniform(jax.random.fold_in(jax.random.fold_in(stream_key, 6), position), (parts,), jnp.float32, low / len(cuts), top_value / len(cuts))
        loudness = loudness * jnp.repeat(jnp.exp(heights), shape[position] // parts).reshape((-1,) + (1,) * (len(shape) - 1 - position))
    return loudness


def gaussian(own_key, extent, scale, reach, shards=(), kind=jnp.bfloat16):
    level = level_of(own_key, extent, shards, -0.22, 0.18) if shards else 1.0
    drawn = jax.random.normal(own_key, extent, jnp.float32) * scale * level
    return jnp.minimum(jnp.maximum(drawn, -reach), reach).astype(kind)


def setup_inputs(seed: int = 0) -> dict:
    seeds = jax.random.split(jax.random.key(seed), 10)
    return {
        "sigma_top": draw_sigma_top(jax.random.fold_in(seeds[9], 71), 0),
        "panel_top": gaussian(seeds[1], (STRUCT, NTOP * ORDER), (2 * STRUCT) ** -0.5, 0.125, ((1, 32),), jnp.float32),
        "diag_top": draw_diag_top(jax.random.fold_in(seeds[9], 71), 0),
        "panel_mid": gaussian(seeds[3], (STRUCT, NMID * ORDER), (2 * STRUCT) ** -0.5, 0.125, ((1, 128),), jnp.float32),
        "diag_mid": draw_diag_mid(jax.random.fold_in(seeds[9], 71), 0),
        "pattern_mid": draw_pattern_mid(jax.random.fold_in(seeds[9], 71), 0),
        "panel_low": gaussian(seeds[6], (STRUCT, NLOW * ORDER), (2 * STRUCT) ** -0.5, 0.125, ((1, 128),), jnp.float32),
        "diag_low": draw_diag_low(jax.random.fold_in(seeds[9], 71), 0),
        "pattern_low": draw_pattern_low(jax.random.fold_in(seeds[9], 71), 0),
    }


HIGH = lax.Precision.HIGHEST


def block_diagonal(blocks):
    block_count = blocks.shape[0]
    block_side = blocks.shape[1]
    eye_table = jnp.eye(block_count, dtype=blocks.dtype)
    spread_out = blocks[:, :, None, :] * eye_table[:, None, :, None]
    return spread_out.reshape(block_count * block_side, block_count * block_side)


def level_panel(inputs):
    covariance, panel_cols, diag_blocks = inputs
    cover_cols = -jnp.dot(covariance, panel_cols, precision=HIGH, preferred_element_type=jnp.float32)
    terms = jnp.einsum("sai,saj->aij", panel_cols.reshape(STRUCT, NBLOCK, BLOCK), cover_cols.reshape(STRUCT, NBLOCK, BLOCK), precision=HIGH)
    return cover_cols, diag_blocks - terms.reshape(NBLOCK * BLOCK, BLOCK)


def child_cov(inputs):
    parent_cov, parent_panel, parent_diag, wanted = inputs
    chosen = jnp.take(parent_panel.reshape(STRUCT, NBLOCK, BLOCK), wanted, axis=1).reshape(STRUCT, STRUCT_BLOCKS * BLOCK)
    chosen_diag = jnp.take(parent_diag.reshape(NBLOCK, BLOCK, BLOCK), wanted, axis=0)
    product = jnp.dot(parent_cov, chosen, precision=HIGH, preferred_element_type=jnp.float32)
    return jnp.dot(chosen.T, product, precision=HIGH, preferred_element_type=jnp.float32) + block_diagonal(chosen_diag)


def flat_cover(cover_stack):
    return jnp.transpose(cover_stack, (1, 0, 2)).reshape(STRUCT, -1)


def reference(sigma_top, panel_top, diag_top, panel_mid, diag_mid, pattern_mid, panel_low, diag_low, pattern_low):
    top_count = sigma_top.shape[0] // STRUCT
    mid_count = pattern_mid.shape[0]
    low_count = pattern_low.shape[0]
    top_cov = sigma_top.reshape(top_count, STRUCT, STRUCT)
    top_panel = jnp.transpose(panel_top.reshape(STRUCT, top_count, ORDER), (1, 0, 2))
    top_diag = diag_top.reshape(top_count, ORDER, BLOCK)
    top_cover, top_marg = lax.map(level_panel, (top_cov, top_panel, top_diag))
    parent_mid = jnp.arange(mid_count, dtype=jnp.int32) // 2
    mid_cov = lax.map(child_cov, (top_cov[parent_mid], top_panel[parent_mid], top_diag[parent_mid], pattern_mid))
    mid_panel = jnp.transpose(panel_mid.reshape(STRUCT, mid_count, ORDER), (1, 0, 2))
    mid_diag = diag_mid.reshape(mid_count, ORDER, BLOCK)
    mid_cover, mid_marg = lax.map(level_panel, (mid_cov, mid_panel, mid_diag))
    parent_low = jnp.arange(low_count, dtype=jnp.int32) // 2
    low_cov = lax.map(child_cov, (mid_cov[parent_low], mid_panel[parent_low], mid_diag[parent_low], pattern_low))
    low_panel = jnp.transpose(panel_low.reshape(STRUCT, low_count, ORDER), (1, 0, 2))
    low_diag = diag_low.reshape(low_count, ORDER, BLOCK)
    low_cover, low_marg = lax.map(level_panel, (low_cov, low_panel, low_diag))
    return (flat_cover(top_cover), top_marg.reshape(-1, BLOCK), flat_cover(mid_cover), mid_marg.reshape(-1, BLOCK), flat_cover(low_cover), low_marg.reshape(-1, BLOCK))
```

```python
import jax
import jax.numpy as jnp
from jax import lax
from jax.sharding import PartitionSpec as P

HIGH = lax.Precision.HIGH
F32 = jnp.float32
B = 256
H = 128


def shift(value, step):
    n = lax.axis_size("rows")
    return lax.ppermute(value, "rows", [(i, (i + step) % n) for i in range(n)])


def partner(value, bit):
    n = lax.axis_size("leaf")
    return lax.ppermute(value, "leaf", [(i, i ^ (1 << bit)) for i in range(n)])


def dot(a, b):
    return jnp.dot(a, b, precision=HIGH, preferred_element_type=F32)


def dot_t(a, b):
    return lax.dot_general(a, b, (((0,), (0,)), ((), ())), precision=HIGH, preferred_element_type=F32)


def pick(pieces, number):
    out = jnp.zeros_like(pieces[0])
    for i, piece in enumerate(pieces):
        out = jnp.where(number == i, piece, out)
    return out


def pack(d):
    a, b, c = d[:H, :H], d[:H, H:], d[H:, H:]
    row = lax.broadcasted_iota(jnp.int32, (H, H), 0)
    col = lax.broadcasted_iota(jnp.int32, (H, H), 1)
    fold = jnp.where(col >= row, a, c)
    diag = jnp.sum(jnp.where(col == row, c, 0.0), axis=0, keepdims=True)
    low = jnp.pad(diag, ((0, 7), (0, H)))
    return jnp.concatenate([jnp.concatenate([b, fold], 1), low], 0)


def unpack(p):
    b, fold, diag = p[:H, :H], p[:H, H:], p[H : H + 1, :H]
    row = lax.broadcasted_iota(jnp.int32, (H, H), 0)
    col = lax.broadcasted_iota(jnp.int32, (H, H), 1)
    turned = fold.T
    a = jnp.where(col >= row, fold, turned)
    c = jnp.where(col == row, diag, jnp.where(col < row, fold, turned))
    return jnp.concatenate([jnp.concatenate([a, b], 1), jnp.concatenate([b.T, c], 1)], 0)


def ordered(stack, x):
    return [lax.dynamic_index_in_dim(stack, (k - x) % 4, 0, False) for k in range(4)]


def child_cov(cov, chosen, diag):
    inner = dot_t(chosen, dot(cov, chosen))
    full = []
    for k in range(4):
        zeros = [jnp.zeros((B, B), F32)] * 4
        zeros[k] = diag[k]
        full.append(jnp.concatenate(zeros, 1))
    return inner + jnp.concatenate(full, 0)


def marg_terms(panel, cross):
    return jnp.concatenate(
        [dot_t(panel[:, a : a + B], cross[:, a : a + B]) for a in range(0, panel.shape[1], B)], 0
    )


def ring_gather(own, x):
    half = own.shape[0] // 16 * 8
    left = shift(own, 1)
    right = shift(own, -1)
    far = jnp.concatenate([shift(left[:half], 1), shift(right[half:], -1)], 0)
    return jnp.stack([own, right, far, left])


def ring_sum(parcels, x):
    half = parcels[2].shape[0] // 16 * 8
    low = shift(parcels[2][:half], 1)
    high = shift(parcels[2][half:], -1)
    up = jnp.concatenate([parcels[1][:half] + low, parcels[1][half:]], 0)
    down = jnp.concatenate([parcels[3][:half], parcels[3][half:] + high], 0)
    return parcels[0] + shift(up, 1) + shift(down, -1)


def local(
    sigma_top, panel_top, diag_top, panel_mid, diag_mid, pattern_mid, panel_low, diag_low, pattern_low
):
    leaf = lax.axis_index("leaf")
    x = lax.axis_index("rows")
    core = leaf % 2
    side = leaf // 2 % 2
    place = leaf % 4
    mid = leaf // 2
    struct = panel_top.shape[0]
    half = struct // 2

    mid_other, diag_mid_other = partner((panel_mid, diag_mid), 0)
    n_mid = panel_mid.shape[1] // B
    packs = [pack(diag_mid[i * B : (i + 1) * B]) for i in range(n_mid)]
    packs += [pack(diag_mid_other[i * B : (i + 1) * B]) for i in range(n_mid)]
    blocks = [panel_mid[:, i * B : (i + 1) * B] for i in range(n_mid)]
    blocks += [mid_other[:, i * B : (i + 1) * B] for i in range(n_mid)]

    n_top = panel_top.shape[1] // B
    own_rows = jnp.where(core == 0, panel_top[:half], panel_top[half:])
    other_rows = jnp.where(core == 0, panel_top[half:], panel_top[:half])

    def top_slot(rows, child):
        b = lax.dynamic_slice(pattern_mid, (child, x), (1, 1))[0, 0]
        number = jnp.where(b // n_top == place, b % n_top, -1)
        return pick([rows[:, i * B : (i + 1) * B] for i in range(n_top)], number)

    own_diag_rows = [diag_top[i * B : (i + 1) * B] for i in range(n_top)]

    def top_diag(child, which):
        out = []
        for k in range(4):
            b = lax.dynamic_slice(pattern_mid, (child, jnp.int32(k)), (1, 1))[0, 0]
            number = jnp.where(b // n_top == place, b % n_top, -1)
            out.append(pick([jnp.where(which == 0, d[:H], d[H:]) for d in own_diag_rows], number))
        return jnp.concatenate(out, 0)

    child_own, child_far = mid, mid ^ 1
    to_core = (top_slot(other_rows, child_own), top_slot(other_rows, child_far))
    from_core = partner(to_core, 0)
    part_own = top_slot(own_rows, child_own) + from_core[0]
    part_far = top_slot(own_rows, child_far) + from_core[1]
    part = part_own + partner(part_far, 1)

    quad = jnp.where(side == 0, sigma_top[:, :half], sigma_top[:, half:])
    quad_far = partner(quad, 1)

    d_core = partner((top_diag(child_own, 1 - core), top_diag(child_far, 1 - core)), 0)
    d_own = top_diag(child_own, core) + d_core[0]
    d_far = top_diag(child_far, core) + d_core[1]
    d_part = d_own + partner(d_far, 1)

    top_parts = ring_gather(part, x)

    def low_slot(d):
        b = lax.dynamic_slice(pattern_low, (leaf, (x + d) % 4), (1, 1))[0, 0]
        spot = b // n_mid
        number = jnp.where(spot % 4 == x, b % n_mid + jnp.where(spot // 4 == core, 0, n_mid), -1)
        return jnp.concatenate([pick(blocks, number), pick(packs, number)], 0)

    low_own = ring_sum([low_slot(d) for d in range(4)], x)
    low_parts = ring_gather(low_own, x)

    sig_core, quad_core = partner((sigma_top, quad_far), 0)
    first, second = jnp.where(core == 0, sigma_top, sig_core), jnp.where(core == 0, sig_core, sigma_top)
    rows_own = jnp.concatenate([first, second], 0)
    far = jnp.concatenate(
        [jnp.where(core == 0, quad_far, quad_core), jnp.where(core == 0, quad_core, quad_far)], 0
    )
    off = jnp.where(side == 0, rows_own[:, half:], rows_own[:, :half])
    near = jnp.where(side == 0, rows_own[:, :half], rows_own[:, half:])
    turned = off.T
    sigma = jnp.concatenate(
        [
            jnp.concatenate([jnp.where(side == 0, near, far), jnp.where(side == 0, off, turned)], 1),
            jnp.concatenate([jnp.where(side == 0, turned, off), jnp.where(side == 0, far, near)], 1),
        ],
        0,
    )

    share = struct // 4
    cross_top = -dot(lax.dynamic_slice_in_dim(sigma, x * share, share, 0), panel_top)
    cols = pick([panel_top[:, 384 * i : 384 * (i + 1)] for i in range(4)], x)
    prod = dot(sigma, cols)
    b0 = pick([panel_top[:, b * B : (b + 1) * B] for b in (0, 1, 3, 4)], x)
    b1 = pick([panel_top[:, b * B : (b + 1) * B] for b in (0, 2, 3, 5)], x)
    b2 = pick([panel_top[:, b * B : (b + 1) * B] for b in (1, 2, 4, 5)], x)
    marg = jnp.concatenate(
        [dot_t(prod[:, :H], b0), dot_t(prod[:, H : 2 * H], b1), dot_t(prod[:, 2 * H :], b2)], 0
    )
    marginal_top = lax.dynamic_slice_in_dim(diag_top, x * 384, 384, 0) + marg

    pair_parts, d_pair = partner((top_parts, d_part), 0)
    upper = jnp.where(core == 0, top_parts, pair_parts)
    lower = jnp.where(core == 0, pair_parts, top_parts)
    chosen = jnp.concatenate(ordered(jnp.concatenate([upper, lower], 1), x), 1)
    d_up, d_low = jnp.where(core == 0, d_part, d_pair), jnp.where(core == 0, d_pair, d_part)
    d_chosen = [
        jnp.concatenate([d_up[k * H : (k + 1) * H], d_low[k * H : (k + 1) * H]], 0) for k in range(4)
    ]
    mid_cov = child_cov(sigma, chosen, d_chosen)
    cross_mid = -dot(mid_cov, panel_mid)
    marginal_mid = diag_mid - marg_terms(panel_mid, cross_mid)

    low_list = ordered(low_parts, x)
    low_chosen = jnp.concatenate([p[:struct] for p in low_list], 1)
    low_cov = child_cov(mid_cov, low_chosen, [unpack(p[struct:]) for p in low_list])
    cross_low = -dot(low_cov, panel_low)
    marginal_low = diag_low - marg_terms(panel_low, cross_low)
    return (cross_top, marginal_top, cross_mid, marginal_mid, cross_low, marginal_low)


def solution(mesh):
    return jax.shard_map(
        local,
        mesh=mesh,
        in_specs=(
            P("leaf", None),
            P(None, "leaf"),
            P("leaf", None),
            P(None, ("leaf", "rows")),
            P(("leaf", "rows"), None),
            P(),
            P(None, ("leaf", "rows")),
            P(("leaf", "rows"), None),
            P(),
        ),
        out_specs=(
            P("rows", "leaf"),
            P(("leaf", "rows"), None),
            P(None, ("leaf", "rows")),
            P(("leaf", "rows"), None),
            P(None, ("leaf", "rows")),
            P(("leaf", "rows"), None),
        ),
        check_vma=False,
    )
```

```python
import jax
import jax.numpy as jnp
from jax import lax
from jax.experimental import pallas as pl
from jax.experimental.pallas import tpu as pltpu
from jax.sharding import PartitionSpec as P

F32 = jnp.float32
BF = jnp.bfloat16
B = 256
H = 128
S = 1024
LO = 576
PK = 136
VMEM = 56 * 2**20


def shift(value, step):
    n = lax.axis_size("rows")
    return lax.ppermute(value, "rows", [(i, (i + step) % n) for i in range(n)])


def partner(value, bit):
    n = lax.axis_size("leaf")
    return lax.ppermute(value, "leaf", [(i, i ^ (1 << bit)) for i in range(n)])


def split(v):
    hi = v.astype(BF)
    return hi, (v - hi.astype(F32)).astype(BF)


def mm(a, b):
    return lax.dot_general(a, b, (((1,), (0,)), ((), ())), preferred_element_type=F32)


def mm3(ah, al, bh, bl):
    return mm(ah, bh) + mm(ah, bl) + mm(al, bh)


def chunk(i):
    return pl.ds(pl.multiple_of(i * B, B), B)


def pack(d):
    a, b, c = d[:H, :H], d[:H, H:], d[H:, H:]
    row = lax.broadcasted_iota(jnp.int32, (H, H), 0)
    col = lax.broadcasted_iota(jnp.int32, (H, H), 1)
    fold = jnp.where(col >= row, a, c)
    diag = jnp.sum(jnp.where(col == row, c, 0.0), axis=0, keepdims=True)
    low = jnp.broadcast_to(diag, (PK - H, H))
    return jnp.concatenate(
        [jnp.concatenate([b, fold], 1), jnp.concatenate([low, jnp.zeros_like(low)], 1)], 0
    )


def unpack(p):
    b, fold, diag = p[:H, :H], p[:H, H:], p[H : H + 1, :H]
    row = lax.broadcasted_iota(jnp.int32, (H, H), 0)
    col = lax.broadcasted_iota(jnp.int32, (H, H), 1)
    turned = fold.T
    a = jnp.where(col >= row, fold, turned)
    c = jnp.where(col == row, diag, jnp.where(col < row, fold, turned))
    return jnp.concatenate([jnp.concatenate([a, b], 1), jnp.concatenate([b.T, c], 1)], 0)


def call(kernel, grid, in_specs, out_specs, out_shape, scratch=(), prefetch=1, flops=0, moved=0):
    return pl.pallas_call(
        kernel,
        grid_spec=pltpu.PrefetchScalarGridSpec(
            num_scalar_prefetch=prefetch,
            grid=grid,
            in_specs=in_specs,
            out_specs=out_specs,
            scratch_shapes=scratch,
        ),
        out_shape=out_shape,
        compiler_params=pltpu.CompilerParams(vmem_limit_bytes=VMEM),
        cost_estimate=pl.CostEstimate(flops=flops, bytes_accessed=moved, transcendentals=0),
    )


def whole(shape):
    return pl.BlockSpec(shape, lambda g, *_: (0,) * len(shape))


def shape(*dims, dtype=F32):
    return jax.ShapeDtypeStruct(dims, dtype)


def top_entry(ids, pattern, far, slot):
    child = ids[0] // 2
    return pattern[child + far * (1 - 2 * (child % 2)), slot]


def select_top(ids, pattern, panel, diag):
    n = panel.shape[1] // B
    half = S // 2

    def panel_spec(far, other):
        def index(g, ids, pattern):
            c = ids[0] % 2
            return (1 - c if other else c), top_entry(ids, pattern, far, ids[1]) % n

        return pl.BlockSpec((half, B), index)

    def diag_spec(far, slot):
        return pl.BlockSpec((B, B), lambda g, ids, pattern: (top_entry(ids, pattern, far, slot) % n, 0))

    def kernel(ids, pattern, *refs):
        pan, dia, (to, keep_own, keep_far, d_own, d_far) = refs[:4], refs[4:12], refs[12:]
        place = ids[0] % 4

        def held(far, slot, v):
            return jnp.where(top_entry(ids, pattern, far, slot) // n == place, v, 0.0)

        to[:half] = held(0, ids[1], pan[0][...])
        to[half:] = held(1, ids[1], pan[1][...])
        keep_own[...] = held(0, ids[1], pan[2][...])
        keep_far[...] = held(1, ids[1], pan[3][...])
        for slot in range(4):
            rows = pl.ds(slot * PK, PK)
            d_own[rows] = held(0, slot, pack(dia[slot][...]))
            d_far[rows] = held(1, slot, pack(dia[4 + slot][...]))

    outs = [(S, B), (half, B), (half, B), (4 * PK, B), (4 * PK, B)]
    return call(
        kernel,
        (1,),
        [panel_spec(0, True), panel_spec(1, True), panel_spec(0, False), panel_spec(1, False)]
        + [diag_spec(far, slot) for far in range(2) for slot in range(4)],
        [whole(o) for o in outs],
        [shape(*o) for o in outs],
        prefetch=2,
        flops=4 * 2**20,
        moved=2**23,
    )(ids, pattern, *[panel] * 4, *[diag] * 8)


def ring_step(g):
    return jnp.where(g == 0, 2, jnp.where(g == 1, 1, jnp.where(g == 2, 3, 0)))


def low_entry(ids, pattern, g):
    return pattern[ids[0], (ids[1] + ring_step(g)) % 4]


def select_low(ids, pattern, panel, panel_other, diag, diag_other):
    n = panel.shape[1] // B

    def kernel(ids, pattern, mine, other, d_mine, d_other, *outs):
        g = pl.program_id(0)
        b = low_entry(ids, pattern, g)
        spot = b // n
        here = spot % 4 == ids[1]
        own = spot // 4 == ids[0] % 2
        for t in range(4):

            @pl.when(g == t)
            def _(t=t):
                low, high = outs[2 * t], outs[2 * t + 1]

                def chosen(u, v):
                    return jnp.where(here, jnp.where(own, u, v), 0.0)

                low[...] = chosen(mine[:LO], other[:LO])
                high[: S - LO] = chosen(mine[LO:], other[LO:])
                high[S - LO :] = pack(chosen(d_mine[...], d_other[...]))

    cols = pl.BlockSpec((S, B), lambda g, ids, pattern: (0, low_entry(ids, pattern, g) % n))
    rows = pl.BlockSpec((B, B), lambda g, ids, pattern: (low_entry(ids, pattern, g) % n, 0))
    outs = [(LO, B), (S - LO + PK, B)] * 4
    return call(
        kernel,
        (4,),
        [cols, cols, rows, rows],
        [whole(o) for o in outs],
        [shape(*o) for o in outs],
        prefetch=2,
        flops=4 * 2**20,
        moved=14 * 2**20,
    )(ids, pattern, panel, panel_other, diag, diag_other)


def join_sigma(ids, own, own_core, far, far_core):
    def kernel(ids, own, own_core, far, far_core, hi, lo):
        side, core = ids[0] // 2 % 2, ids[0] % 2
        near_half = pl.ds(pl.multiple_of(side * 512, 512), 512)
        far_half = pl.ds(pl.multiple_of((1 - side) * 512, 512), 512)
        for ref, quad, c in ((own, far, core), (own_core, far_core, 1 - core)):
            rows = chunk(2 * side + c)
            hi[rows, :], lo[rows, :] = split(ref[...])
            hi[far_half, rows], lo[far_half, rows] = split(ref[:, far_half].T)
            rows = chunk(2 * (1 - side) + c)
            hi[rows, far_half], lo[rows, far_half] = split(quad[...])

    return call(
        kernel,
        (1,),
        [whole((B, S)), whole((B, S)), whole((B, 512)), whole((B, 512))],
        [whole((S, S))] * 2,
        [shape(S, S, dtype=BF)] * 2,
        flops=2**23,
        moved=7 * 2**20,
    )(ids, own, own_core, far, far_core)


def top_level(ids, hi, lo, panel, diag):
    n = panel.shape[1] // B

    def kernel(ids, hi, lo, panel, diag, cross, marg):
        g = pl.program_id(0)
        x = ids[1]
        first = x // 2 * 3 + x % 2
        uh, ul = split(panel[...])
        mine = chunk(x)
        cross[...] = -mm3(hi[mine, :], lo[mine, :], uh, ul)

        @pl.when((g == first) | (g == first + 1))
        def _():
            yh, yl = split(mm3(hi[...], lo[...], uh, ul))
            th, tl = split(panel[...].T)
            term = diag[...] + mm3(th, tl, yh, yl)

            @pl.when((x % 2 == 0) & (g == first))
            def _():
                marg[:B] = term

            @pl.when((x % 2 == 0) & (g != first))
            def _():
                marg[B:] = term[:H]

            @pl.when((x % 2 == 1) & (g == first))
            def _():
                marg[:H] = term[H:]

            @pl.when((x % 2 == 1) & (g != first))
            def _():
                marg[H:] = term

    return call(
        kernel,
        (n,),
        [
            whole((S, S)),
            whole((S, S)),
            pl.BlockSpec((S, B), lambda g, *_: (0, g)),
            pl.BlockSpec((B, B), lambda g, *_: (g, 0)),
        ],
        [pl.BlockSpec((B, B), lambda g, *_: (0, g)), whole((B + H, B))],
        [shape(B, n * B), shape(B + H, B)],
        flops=5 * 2**30,
        moved=13 * 2**20,
    )(ids, hi, lo, panel, diag)


def form_cov(hi, lo, uh, ul, th, tl, ph, pl_, jh, jl, place_slot, diag_of):
    for d in range(4):
        place_slot(d)

    @pl.loop(0, 4)
    def _(n):
        at = chunk(n)
        ph[:, at], pl_[:, at] = split(mm3(th[...], tl[...], hi[:, at], lo[:, at]))

    for n in range(4):
        at = slice(n * B, (n + 1) * B)
        jh_n = mm3(ph[...], pl_[...], uh[:, at], ul[:, at])
        for k in range(4):
            rows = slice(k * B, (k + 1) * B)
            value = jh_n[rows] + diag_of(n) if k == n else jh_n[rows]
            jh[rows, at], jl[rows, at] = split(value)


def level_step(jh, jl, panel, diag, cross, marg):
    uh, ul = split(panel[...])
    value = -mm3(jh[...], jl[...], uh, ul)
    cross[...] = value
    xh, xl = split(value)
    th, tl = split(panel[...].T)
    marg[...] = diag[...] - mm3(th, tl, xh, xl)


def level_specs(n):
    cols = pl.BlockSpec((S, B), lambda g, *_: (0, g))
    rows = pl.BlockSpec((B, B), lambda g, *_: (g, 0))
    return [cols, rows], [cols, rows], [shape(S, n * B), shape(n * B, B)]


def mid_level(ids, hi, lo, parts, parts_core, d_own, d_core, panel, diag):
    n = panel.shape[1] // B
    k = len(parts)

    def kernel(ids, hi, lo, *refs):
        own, core, (d0, d1, panel, diag, cross, marg, jh, jl) = refs[:k], refs[k : 2 * k], refs[2 * k : 2 * k + 8]
        uh, ul, th, tl, ph, pq = refs[2 * k + 8 :]
        x, c = ids[1], ids[0] % 2

        def place_slot(d):
            at = chunk((x + d) % 4)
            for refs_, which in ((own, c), (core, 1 - c)):
                base = which * 512
                if d == 2:
                    pieces = ((refs_[2], 0, 256), (refs_[3], 256, 256))
                else:
                    pieces = ((refs_[{0: 0, 1: 1, 3: 4}[d]], 0, 512),)
                for ref, off, size in pieces:
                    rows = pl.ds(pl.multiple_of(base + off, 256), size)
                    v = ref[...]
                    uh[rows, at], ul[rows, at] = split(v)
                    th[at, rows], tl[at, rows] = split(v.T)

        def diag_of(s):
            rows = slice(s * PK, (s + 1) * PK)
            return unpack(d0[rows] + d1[rows])

        @pl.when(pl.program_id(0) == 0)
        def _():
            form_cov(hi, lo, uh, ul, th, tl, ph, pq, jh, jl, place_slot, diag_of)

        level_step(jh, jl, panel, diag, cross, marg)

    ins, outs, shapes = level_specs(n)
    return call(
        kernel,
        (n,),
        [whole((S, S))] * 2
        + [whole(p.shape) for p in (*parts, *parts_core)]
        + [whole((4 * PK, B))] * 2
        + ins,
        outs + [whole((S, S))] * 2,
        shapes + [shape(S, S, dtype=BF)] * 2,
        [pltpu.VMEM((S, S), BF)] * 6,
        flops=3 * 7 * 2**30,
        moved=20 * 2**20,
    )(ids, hi, lo, *parts, *parts_core, d_own, d_core, panel, diag)


def low_level(ids, hi, lo, parts, panel, diag):
    n = panel.shape[1] // B

    def kernel(ids, hi, lo, *refs):
        part, (panel, diag, cross, marg) = refs[:8], refs[8:12]
        uh, ul, th, tl, ph, pq, jh, jl, dd = refs[12:]
        x = ids[1]

        def place_slot(d):
            slot = (x + d) % 4
            at = chunk(slot)
            v = jnp.concatenate([part[2 * d][...], part[2 * d + 1][: S - LO]], 0)
            uh[:, at], ul[:, at] = split(v)
            th[at, :], tl[at, :] = split(v.T)
            dd[slot] = part[2 * d + 1][S - LO :]

        @pl.when(pl.program_id(0) == 0)
        def _():
            form_cov(hi, lo, uh, ul, th, tl, ph, pq, jh, jl, place_slot, lambda s: unpack(dd[s]))

        level_step(jh, jl, panel, diag, cross, marg)

    ins, outs, shapes = level_specs(n)
    return call(
        kernel,
        (n,),
        [whole((S, S))] * 2 + [whole(p.shape) for p in parts] + ins,
        outs,
        shapes,
        [pltpu.VMEM((S, S), BF)] * 8 + [pltpu.VMEM((4, PK, B), F32)],
        flops=3 * 9 * 2**30,
        moved=26 * 2**20,
    )(ids, hi, lo, *parts, panel, diag)


def local(
    sigma_top, panel_top, diag_top, panel_mid, diag_mid, pattern_mid, panel_low, diag_low, pattern_low
):
    leaf = lax.axis_index("leaf")
    x = lax.axis_index("rows")
    ids = jnp.stack([leaf, x]).astype(jnp.int32)
    side = leaf // 2 % 2
    half = S // 2

    panel_other, diag_other = partner((panel_mid, diag_mid), 0)
    to_core, keep_own, keep_far, d_keep, d_far = select_top(ids, pattern_mid, panel_top, diag_top)
    from_core = partner(to_core, 0)
    sig_core = partner(sigma_top, 0)
    quad = jnp.where(side == 0, sigma_top[:, :half], sigma_top[:, half:])

    part = keep_own + from_core[:half] + partner(keep_far + from_core[half:], 1)
    quad_far = partner(quad, 1)
    d_part = d_keep + partner(d_far, 1)

    two_lo, two_hi, one_lo, one_hi, three_lo, three_hi, own_lo, own_hi = select_low(
        ids, pattern_low, panel_mid, panel_other, diag_mid, diag_other
    )
    r_two_lo = shift(two_lo, 1)
    r_two_hi = shift(two_hi, -1)
    r_one_hi = shift(one_hi, 1)
    r_three_lo = shift(three_lo, -1)
    r_one_lo = shift(one_lo + r_two_lo, 1)
    r_three_hi = shift(three_hi + r_two_hi, -1)

    left = shift(part, 1)
    right = shift(part, -1)
    far_a = shift(left[:B], 1)
    far_b = shift(right[B:], -1)
    parts = [part, right, far_a, far_b, left]
    parts_core = [partner(p, 0) for p in parts]

    own_lo = own_lo + r_one_lo + r_three_lo
    own_hi = own_hi + r_one_hi + r_three_hi
    left_lo, right_lo = shift(own_lo, 1), shift(own_lo, -1)
    right_hi, left_hi = shift(own_hi, -1), shift(own_hi, 1)
    far_lo = shift(left_lo, 1)
    far_hi = shift(right_hi, -1)

    quad_core = partner(quad_far, 0)
    d_core = partner(d_part, 0)
    hi, lo = join_sigma(ids, sigma_top, sig_core, quad_far, quad_core)
    cross_top, marginal_top = top_level(ids, hi, lo, panel_top, diag_top)
    cross_mid, marginal_mid, mid_hi, mid_lo = mid_level(
        ids, hi, lo, parts, parts_core, d_part, d_core, panel_mid, diag_mid
    )
    cross_low, marginal_low = low_level(
        ids,
        mid_hi,
        mid_lo,
        [own_lo, own_hi, right_lo, right_hi, far_lo, far_hi, left_lo, left_hi],
        panel_low,
        diag_low,
    )
    return (cross_top, marginal_top, cross_mid, marginal_mid, cross_low, marginal_low)


def solution(mesh):
    return jax.shard_map(
        local,
        mesh=mesh,
        in_specs=(
            P("leaf", None),
            P(None, "leaf"),
            P("leaf", None),
            P(None, ("leaf", "rows")),
            P(("leaf", "rows"), None),
            P(),
            P(None, ("leaf", "rows")),
            P(("leaf", "rows"), None),
            P(),
        ),
        out_specs=(
            P("rows", "leaf"),
            P(("leaf", "rows"), None),
            P(None, ("leaf", "rows")),
            P(("leaf", "rows"), None),
            P(None, ("leaf", "rows")),
            P(("leaf", "rows"), None),
        ),
        check_vma=False,
    )
```

```python
import jax
import jax.numpy as jnp
from jax import lax
from jax.experimental import pallas as pl
from jax.experimental.pallas import tpu as pltpu
from jax.sharding import PartitionSpec as P

F32 = jnp.float32
BF = jnp.bfloat16
B = 256
H = 128
S = 1024
LO = 576
PK = 136
HI = S - LO + PK
VMEM = 56 * 2**20


def shift(value, step):
    n = lax.axis_size("rows")
    return lax.ppermute(value, "rows", [(i, (i + step) % n) for i in range(n)])


def partner(value, bit):
    n = lax.axis_size("leaf")
    return lax.ppermute(value, "leaf", [(i, i ^ (1 << bit)) for i in range(n)])


def tie(*values):
    return lax.optimization_barrier(values)


def split(v):
    hi = v.astype(BF)
    return hi, (v - hi.astype(F32)).astype(BF)


def mm(a, b):
    return lax.dot_general(a, b, (((1,), (0,)), ((), ())), preferred_element_type=F32)


def mm3(ah, al, bh, bl):
    return mm(ah, bh) + mm(ah, bl) + mm(al, bh)


def chunk(i):
    return pl.ds(pl.multiple_of(i * B, B), B)


def pack(d):
    a, b, c = d[:H, :H], d[:H, H:], d[H:, H:]
    row = lax.broadcasted_iota(jnp.int32, (H, H), 0)
    col = lax.broadcasted_iota(jnp.int32, (H, H), 1)
    fold = jnp.where(col >= row, a, c)
    diag = jnp.sum(jnp.where(col == row, c, 0.0), axis=0, keepdims=True)
    low = jnp.broadcast_to(diag, (PK - H, H))
    return jnp.concatenate(
        [jnp.concatenate([b, fold], 1), jnp.concatenate([low, jnp.zeros_like(low)], 1)], 0
    )


def unpack(p):
    b, fold, diag = p[:H, :H], p[:H, H:], p[H : H + 1, :H]
    row = lax.broadcasted_iota(jnp.int32, (H, H), 0)
    col = lax.broadcasted_iota(jnp.int32, (H, H), 1)
    turned = fold.T
    a = jnp.where(col >= row, fold, turned)
    c = jnp.where(col == row, diag, jnp.where(col < row, fold, turned))
    return jnp.concatenate([jnp.concatenate([a, b], 1), jnp.concatenate([b.T, c], 1)], 0)


def call(kernel, grid, in_specs, out_specs, out_shape, scratch=(), prefetch=1):
    return pl.pallas_call(
        kernel,
        grid_spec=pltpu.PrefetchScalarGridSpec(
            num_scalar_prefetch=prefetch,
            grid=grid,
            in_specs=in_specs,
            out_specs=out_specs,
            scratch_shapes=scratch,
        ),
        out_shape=out_shape,
        compiler_params=pltpu.CompilerParams(vmem_limit_bytes=VMEM),
        cost_estimate=pl.CostEstimate(flops=1024, bytes_accessed=1024, transcendentals=0),
    )


def whole(shape):
    return pl.BlockSpec(shape, lambda g, *_: (0,) * len(shape))


def shape(*dims, dtype=F32):
    return jax.ShapeDtypeStruct(dims, dtype)


def top_entry(ids, pattern, far, slot):
    child = ids[0] // 2
    return pattern[child + far * (1 - 2 * (child % 2)), slot]


def select_top(ids, pattern, panel, diag, far):
    n = panel.shape[1] // B
    half = S // 2

    def panel_spec(other):
        def index(g, ids, pattern):
            c = ids[0] % 2
            return (1 - c if other else c), top_entry(ids, pattern, far, g) % n

        return pl.BlockSpec((half, B), index)

    def kernel(ids, pattern, p0, p1, dia, to, keep, d):
        held = top_entry(ids, pattern, far, pl.program_id(0)) // n == ids[0] % 4
        to[...] = jnp.where(held, p0[...], 0.0)
        keep[...] = jnp.where(held, p1[...], 0.0)
        d[...] = jnp.where(held, pack(dia[...]), 0.0)

    wide = pl.BlockSpec((half, B), lambda g, *_: (0, g))
    tall = pl.BlockSpec((PK, B), lambda g, *_: (g, 0))
    rows = pl.BlockSpec((B, B), lambda g, ids, pattern: (top_entry(ids, pattern, far, g) % n, 0))
    return call(
        kernel,
        (4,),
        [panel_spec(True), panel_spec(False), rows],
        [wide, wide, tall],
        [shape(half, S), shape(half, S), shape(4 * PK, B)],
        prefetch=2,
    )(ids, pattern, panel, panel, diag)


def ring_step(g):
    return jnp.where(g == 0, 2, jnp.where(g == 1, 1, jnp.where(g == 2, 3, 0)))


def low_entry(ids, pattern, g):
    return pattern[ids[0], (ids[1] + ring_step(g)) % 4]


def select_low(ids, pattern, panel, panel_other, diag, diag_other):
    n = panel.shape[1] // B

    def kernel(ids, pattern, mine, other, d_mine, d_other, plus, minus, one_lo, three_hi, own_lo, own_hi):
        g = pl.program_id(0)
        b = low_entry(ids, pattern, g)
        spot = b // n
        here = spot % 4 == ids[1]
        own = spot // 4 == ids[0] % 2
        lows = (plus.at[:LO], one_lo, minus.at[HI:], own_lo)
        highs = (minus.at[:HI], plus.at[LO:], three_hi, own_hi)
        for t in range(4):

            @pl.when(g == t)
            def _(t=t):
                low, high = lows[t], highs[t]

                def chosen(u, v):
                    return jnp.where(here, jnp.where(own, u, v), 0.0)

                low[...] = chosen(mine[:LO], other[:LO])
                high[: S - LO] = chosen(mine[LO:], other[LO:])
                high[S - LO :] = pack(chosen(d_mine[...], d_other[...]))

    cols = pl.BlockSpec((S, B), lambda g, ids, pattern: (0, low_entry(ids, pattern, g) % n))
    rows = pl.BlockSpec((B, B), lambda g, ids, pattern: (low_entry(ids, pattern, g) % n, 0))
    outs = [(LO + HI, B), (LO + HI, B), (LO, B), (HI, B), (LO, B), (HI, B)]
    return call(
        kernel,
        (4,),
        [cols, cols, rows, rows],
        [whole(o) for o in outs],
        [shape(*o) for o in outs],
        prefetch=2,
    )(ids, pattern, panel, panel_other, diag, diag_other)


def join_sigma(ids, own, own_core, far, far_core):
    def kernel(ids, own, own_core, far, far_core, hi, lo):
        side, core = ids[0] // 2 % 2, ids[0] % 2
        near_half = pl.ds(pl.multiple_of(side * 512, 512), 512)
        far_half = pl.ds(pl.multiple_of((1 - side) * 512, 512), 512)
        for ref, quad, c in ((own, far, core), (own_core, far_core, 1 - core)):
            rows = chunk(2 * side + c)
            hi[rows, :], lo[rows, :] = split(ref[...])
            hi[far_half, rows], lo[far_half, rows] = split(ref[:, far_half].T)
            rows = chunk(2 * (1 - side) + c)
            hi[rows, far_half], lo[rows, far_half] = split(quad[...])

    return call(
        kernel,
        (1,),
        [whole((B, S)), whole((B, S)), whole((B, 512)), whole((B, 512))],
        [whole((S, S))] * 2,
        [shape(S, S, dtype=BF)] * 2,
    )(ids, own, own_core, far, far_core)


def top_level(ids, hi, lo, panel, diag):
    n = panel.shape[1] // B

    def kernel(ids, hi, lo, panel, diag, cross, marg):
        g = pl.program_id(0)
        x = ids[1]
        first = x // 2 * 3 + x % 2
        uh, ul = split(panel[...])
        mine = chunk(x)
        cross[...] = -mm3(hi[mine, :], lo[mine, :], uh, ul)

        @pl.when((g == first) | (g == first + 1))
        def _():
            yh, yl = split(mm3(hi[...], lo[...], uh, ul))
            th, tl = split(panel[...].T)
            term = diag[...] + mm3(th, tl, yh, yl)

            @pl.when((x % 2 == 0) & (g == first))
            def _():
                marg[:B] = term

            @pl.when((x % 2 == 0) & (g != first))
            def _():
                marg[B:] = term[:H]

            @pl.when((x % 2 == 1) & (g == first))
            def _():
                marg[:H] = term[H:]

            @pl.when((x % 2 == 1) & (g != first))
            def _():
                marg[H:] = term

    return call(
        kernel,
        (n,),
        [
            whole((S, S)),
            whole((S, S)),
            pl.BlockSpec((S, B), lambda g, *_: (0, g)),
            pl.BlockSpec((B, B), lambda g, *_: (g, 0)),
        ],
        [pl.BlockSpec((B, B), lambda g, *_: (0, g)), whole((B + H, B))],
        [shape(B, n * B), shape(B + H, B)],
    )(ids, hi, lo, panel, diag)


def form_cov(hi, lo, uh, ul, th, tl, ph, pl_, jh, jl, place_slot, diag_of):
    for d in range(4):
        place_slot(d)

    for n in range(4):
        at = slice(n * B, (n + 1) * B)
        ph[:, at], pl_[:, at] = split(mm3(th[...], tl[...], hi[:, at], lo[:, at]))

    for n in range(4):
        at = slice(n * B, (n + 1) * B)
        above = n * B
        value = mm3(ph[: above + B], pl_[: above + B], uh[:, at], ul[:, at])
        jh[at, at], jl[at, at] = split(value[above:] + diag_of(n))
        if n:
            jh[:above, at], jl[:above, at] = split(value[:above])
            jh[at, :above], jl[at, :above] = split(value[:above].T)


def level_step(jh, jl, panel, diag, cross, marg):
    uh, ul = split(panel[...])
    value = -mm3(jh[...], jl[...], uh, ul)
    cross[...] = value
    xh, xl = split(value)
    th, tl = split(panel[...].T)
    for a in range(panel.shape[1] // B):
        at = slice(a * B, (a + 1) * B)
        both = mm(jnp.concatenate([th[at], tl[at]], 0), xh[:, at])
        marg[at] = diag[at] - (both[:B] + both[B:] + mm(th[at], xl[:, at]))


def level_specs(n, wide):
    cols = pl.BlockSpec((S, wide * B), lambda g, *_: (0, g))
    rows = pl.BlockSpec((wide * B, B), lambda g, *_: (g, 0))
    return [cols, rows], [cols, rows], [shape(S, n * B), shape(n * B, B)]


def mid_level(ids, hi, lo, part, part_core, d_own, d_core, panel, diag):
    n = panel.shape[1] // B

    def kernel(ids, hi, lo, own, core, d0, d1, panel, diag, cross, marg, jh, jl, uh, ul, th, tl, ph, pq):
        c = ids[0] % 2

        def place_slot(d):
            at = slice(d * B, (d + 1) * B)
            for ref, which in ((own, c), (core, 1 - c)):
                rows = pl.ds(pl.multiple_of(which * 512, 512), 512)
                v = ref[:, at]
                uh[rows, at], ul[rows, at] = split(v)
                th[at, rows], tl[at, rows] = split(v.T)

        def diag_of(s):
            rows = slice(s * PK, (s + 1) * PK)
            return unpack(d0[rows] + d1[rows])

        @pl.when(pl.program_id(0) == 0)
        def _():
            form_cov(hi, lo, uh, ul, th, tl, ph, pq, jh, jl, place_slot, diag_of)

        level_step(jh, jl, panel, diag, cross, marg)

    ins, outs, shapes = level_specs(n, n)
    return call(
        kernel,
        (1,),
        [whole((S, S))] * 2
        + [whole(part.shape)] * 2
        + [whole((4 * PK, B))] * 2
        + ins,
        outs + [whole((S, S))] * 2,
        shapes + [shape(S, S, dtype=BF)] * 2,
        [pltpu.VMEM((S, S), BF)] * 6,
    )(ids, hi, lo, part, part_core, d_own, d_core, panel, diag)


def low_level(ids, hi, lo, parts, panel, diag):
    n = panel.shape[1] // B

    def kernel(ids, hi, lo, *refs):
        own_lo, own_hi, left_lo, right_hi, from_left, from_right = refs[:6]
        panel, diag, cross, marg = refs[6:10]
        uh, ul, th, tl, ph, pq, jh, jl, dd = refs[10:]
        x = ids[1]
        lows = (own_lo, from_right.at[:LO], from_left.at[HI:], left_lo)
        highs = (own_hi, right_hi, from_right.at[LO:], from_left.at[:HI])

        def place_slot(d):
            slot = (x + d) % 4
            at = chunk(slot)
            v = jnp.concatenate([lows[d][...], highs[d][: S - LO]], 0)
            uh[:, at], ul[:, at] = split(v)
            th[at, :], tl[at, :] = split(v.T)
            dd[slot] = highs[d][S - LO :]

        @pl.when(pl.program_id(0) == 0)
        def _():
            form_cov(hi, lo, uh, ul, th, tl, ph, pq, jh, jl, place_slot, lambda s: unpack(dd[s]))

        level_step(jh, jl, panel, diag, cross, marg)

    ins, outs, shapes = level_specs(n, 2)
    return call(
        kernel,
        (n // 2,),
        [whole((S, S))] * 2 + [whole(p.shape) for p in parts] + ins,
        outs,
        shapes,
        [pltpu.VMEM((S, S), BF)] * 8 + [pltpu.VMEM((4, PK, B), F32)],
    )(ids, hi, lo, *parts, panel, diag)


def local(
    sigma_top, panel_top, diag_top, panel_mid, diag_mid, pattern_mid, panel_low, diag_low, pattern_low
):
    leaf = lax.axis_index("leaf")
    x = lax.axis_index("rows")
    ids = jnp.stack([leaf, x]).astype(jnp.int32)
    side = leaf // 2 % 2
    half = S // 2

    panel_other, diag_other = partner((panel_mid, diag_mid), 0)
    quad = jnp.where(side == 0, sigma_top[:, :half], sigma_top[:, half:])
    quad_far = partner(quad, 1)
    to_far, keep_far, d_far = select_top(ids, pattern_mid, panel_top, diag_top, 1)
    core_far = partner(to_far, 0)

    plus, minus, one_lo, three_hi, own_lo, own_hi = select_low(
        ids, pattern_low, panel_mid, panel_other, diag_mid, diag_other
    )
    plus, minus, quad_far, sigma_ = tie(plus, minus, quad_far, sigma_top)
    r_plus = shift(plus, 1)
    r_minus = shift(minus, -1)
    sig_core = partner(sigma_, 0)
    quad_core = partner(quad_far, 0)

    far_sum, sig_core = tie(keep_far + core_far, sig_core)
    recv = partner(far_sum, 1)
    hi, lo = join_sigma(ids, sigma_top, sig_core, quad_far, quad_core)
    cross_top, marginal_top = top_level(ids, hi, lo, panel_top, diag_top)
    r_plus, r_minus, cross_top, panel_top_, d_far = tie(r_plus, r_minus, cross_top, panel_top, d_far)
    to_own, keep_own, d_keep = select_top(ids, pattern_mid, panel_top_, diag_top, 0)
    core_own = partner(to_own, 0)
    d_recv = partner(d_far, 1)
    r_one_lo = shift(one_lo + r_plus[:LO], 1)
    r_three_hi = shift(three_hi + r_minus[:HI], -1)
    own_lo = own_lo + r_minus[HI:]
    own_hi = own_hi + r_plus[LO:]

    own_lo = own_lo + r_one_lo
    own_hi = own_hi + r_three_hi
    own_lo, own_hi, keep_own = tie(own_lo, own_hi, keep_own)
    left_lo, right_hi = shift(own_lo, 1), shift(own_hi, -1)

    left_lo, right_hi, recv, d_recv = tie(left_lo, right_hi, recv, d_recv)
    part = keep_own + core_own + recv
    part_core = partner(part, 0)
    d_part = d_keep + d_recv
    d_core = partner(d_part, 0)

    next_plus = jnp.concatenate([own_hi, left_lo], 0)
    next_minus = jnp.concatenate([own_lo, right_hi], 0)
    next_plus, next_minus, hi = tie(next_plus, next_minus, hi)
    from_left = shift(next_plus, 1)
    from_right = shift(next_minus, -1)
    cross_mid, marginal_mid, mid_hi, mid_lo = mid_level(
        ids, hi, lo, part, part_core, d_part, d_core, panel_mid, diag_mid
    )
    cross_low, marginal_low = low_level(
        ids,
        mid_hi,
        mid_lo,
        [own_lo, own_hi, left_lo, right_hi, from_left, from_right],
        panel_low,
        diag_low,
    )
    return (cross_top, marginal_top, cross_mid, marginal_mid, cross_low, marginal_low)


def solution(mesh):
    return jax.shard_map(
        local,
        mesh=mesh,
        in_specs=(
            P("leaf", None),
            P(None, "leaf"),
            P("leaf", None),
            P(None, ("leaf", "rows")),
            P(("leaf", "rows"), None),
            P(),
            P(None, ("leaf", "rows")),
            P(("leaf", "rows"), None),
            P(),
        ),
        out_specs=(
            P("rows", "leaf"),
            P(("leaf", "rows"), None),
            P(None, ("leaf", "rows")),
            P(("leaf", "rows"), None),
            P(None, ("leaf", "rows")),
            P(("leaf", "rows"), None),
        ),
        check_vma=False,
    )
```

```python
import jax
import jax.numpy as jnp
from jax import lax
from jax.experimental import pallas as pl
from jax.experimental.pallas import tpu as pltpu
from jax.sharding import PartitionSpec as P

F32 = jnp.float32
BF = jnp.bfloat16
B = 256
H = 128
S = 1024
LO = 576
PK = 136
HI = S - LO + PK
VMEM = 56 * 2**20


def shift(value, step):
    n = lax.axis_size("rows")
    return lax.ppermute(value, "rows", [(i, (i + step) % n) for i in range(n)])


def partner(value, bit):
    n = lax.axis_size("leaf")
    return lax.ppermute(value, "leaf", [(i, i ^ (1 << bit)) for i in range(n)])


def tie(*values):
    return lax.optimization_barrier(values)


def split(v):
    hi = v.astype(BF)
    return hi, (v - hi.astype(F32)).astype(BF)


def mm(a, b):
    return lax.dot_general(a, b, (((1,), (0,)), ((), ())), preferred_element_type=F32)


def mm3(ah, al, bh, bl):
    return mm(ah, bh) + mm(ah, bl) + mm(al, bh)


def chunk(i):
    return pl.ds(pl.multiple_of(i * B, B), B)


def pack(d):
    a, b, c = d[:H, :H], d[:H, H:], d[H:, H:]
    row = lax.broadcasted_iota(jnp.int32, (H, H), 0)
    col = lax.broadcasted_iota(jnp.int32, (H, H), 1)
    fold = jnp.where(col >= row, a, c)
    diag = jnp.sum(jnp.where(col == row, c, 0.0), axis=0, keepdims=True)
    low = jnp.broadcast_to(diag, (PK - H, H))
    return jnp.concatenate(
        [jnp.concatenate([b, fold], 1), jnp.concatenate([low, jnp.zeros_like(low)], 1)], 0
    )


def unpack(p):
    b, fold, diag = p[:H, :H], p[:H, H:], p[H : H + 1, :H]
    row = lax.broadcasted_iota(jnp.int32, (H, H), 0)
    col = lax.broadcasted_iota(jnp.int32, (H, H), 1)
    turned = fold.T
    a = jnp.where(col >= row, fold, turned)
    c = jnp.where(col == row, diag, jnp.where(col < row, fold, turned))
    return jnp.concatenate([jnp.concatenate([a, b], 1), jnp.concatenate([b.T, c], 1)], 0)


def call(kernel, grid, in_specs, out_specs, out_shape, scratch=(), prefetch=1):
    return pl.pallas_call(
        kernel,
        grid_spec=pltpu.PrefetchScalarGridSpec(
            num_scalar_prefetch=prefetch,
            grid=grid,
            in_specs=in_specs,
            out_specs=out_specs,
            scratch_shapes=scratch,
        ),
        out_shape=out_shape,
        compiler_params=pltpu.CompilerParams(vmem_limit_bytes=VMEM),
        cost_estimate=pl.CostEstimate(flops=1024, bytes_accessed=1024, transcendentals=0),
    )


def whole(shape):
    return pl.BlockSpec(shape, lambda g, *_: (0,) * len(shape))


def shape(*dims, dtype=F32):
    return jax.ShapeDtypeStruct(dims, dtype)


def top_entry(ids, pattern, far, slot):
    child = ids[0] // 2
    return pattern[child + far * (1 - 2 * (child % 2)), slot]


def select_top(ids, pattern, panel, diag, far):
    n = panel.shape[1] // B
    half = S // 2

    def panel_spec(other):
        def index(g, ids, pattern):
            c = ids[0] % 2
            return (1 - c if other else c), top_entry(ids, pattern, far, g) % n

        return pl.BlockSpec((half, B), index)

    def kernel(ids, pattern, p0, p1, dia, to, keep, d):
        held = top_entry(ids, pattern, far, pl.program_id(0)) // n == ids[0] % 4
        to[...] = jnp.where(held, p0[...], 0.0)
        keep[...] = jnp.where(held, p1[...], 0.0)
        d[...] = jnp.where(held, pack(dia[...]), 0.0)

    wide = pl.BlockSpec((half, B), lambda g, *_: (0, g))
    tall = pl.BlockSpec((PK, B), lambda g, *_: (g, 0))
    rows = pl.BlockSpec((B, B), lambda g, ids, pattern: (top_entry(ids, pattern, far, g) % n, 0))
    return call(
        kernel,
        (4,),
        [panel_spec(True), panel_spec(False), rows],
        [wide, wide, tall],
        [shape(half, S), shape(half, S), shape(4 * PK, B)],
        prefetch=2,
    )(ids, pattern, panel, panel, diag)


def ring_step(g):
    return jnp.where(g == 0, 2, jnp.where(g == 1, 1, jnp.where(g == 2, 3, 0)))


def low_entry(ids, pattern, g):
    return pattern[ids[0], (ids[1] + ring_step(g)) % 4]


def select_low(ids, pattern, panel, panel_other, diag, diag_other):
    n = panel.shape[1] // B

    def kernel(ids, pattern, mine, other, d_mine, d_other, plus, minus, one_lo, three_hi, own_lo, own_hi):
        g = pl.program_id(0)
        b = low_entry(ids, pattern, g)
        spot = b // n
        here = spot % 4 == ids[1]
        own = spot // 4 == ids[0] % 2
        lows = (plus.at[:LO], one_lo, minus.at[HI:], own_lo)
        highs = (minus.at[:HI], plus.at[LO:], three_hi, own_hi)
        for t in range(4):

            @pl.when(g == t)
            def _(t=t):
                low, high = lows[t], highs[t]

                def chosen(u, v):
                    return jnp.where(here, jnp.where(own, u, v), 0.0)

                low[...] = chosen(mine[:LO], other[:LO])
                high[: S - LO] = chosen(mine[LO:], other[LO:])
                high[S - LO :] = pack(chosen(d_mine[...], d_other[...]))

    cols = pl.BlockSpec((S, B), lambda g, ids, pattern: (0, low_entry(ids, pattern, g) % n))
    rows = pl.BlockSpec((B, B), lambda g, ids, pattern: (low_entry(ids, pattern, g) % n, 0))
    outs = [(LO + HI, B), (LO + HI, B), (LO, B), (HI, B), (LO, B), (HI, B)]
    return call(
        kernel,
        (4,),
        [cols, cols, rows, rows],
        [whole(o) for o in outs],
        [shape(*o) for o in outs],
        prefetch=2,
    )(ids, pattern, panel, panel_other, diag, diag_other)


def join_sigma(ids, own, own_core, far, far_core):
    def kernel(ids, own, own_core, far, far_core, hi, lo):
        side, core = ids[0] // 2 % 2, ids[0] % 2
        near_half = pl.ds(pl.multiple_of(side * 512, 512), 512)
        far_half = pl.ds(pl.multiple_of((1 - side) * 512, 512), 512)
        for ref, quad, c in ((own, far, core), (own_core, far_core, 1 - core)):
            rows = chunk(2 * side + c)
            hi[rows, :], lo[rows, :] = split(ref[...])
            hi[far_half, rows], lo[far_half, rows] = split(ref[:, far_half].T)
            rows = chunk(2 * (1 - side) + c)
            hi[rows, far_half], lo[rows, far_half] = split(quad[...])

    return call(
        kernel,
        (1,),
        [whole((B, S)), whole((B, S)), whole((B, 512)), whole((B, 512))],
        [whole((S, S))] * 2,
        [shape(S, S, dtype=BF)] * 2,
    )(ids, own, own_core, far, far_core)


def top_level(ids, hi, lo, panel, diag):
    n = panel.shape[1] // B

    def kernel(ids, hi, lo, panel, diag, cross, marg):
        g = pl.program_id(0)
        x = ids[1]
        first = x // 2 * 3 + x % 2
        uh, ul = split(panel[...])
        mine = chunk(x)
        cross[...] = -mm3(hi[mine, :], lo[mine, :], uh, ul)

        @pl.when((g == first) | (g == first + 1))
        def _():
            yh, yl = split(mm3(hi[...], lo[...], uh, ul))
            th, tl = split(panel[...].T)
            term = diag[...] + mm3(th, tl, yh, yl)

            @pl.when((x % 2 == 0) & (g == first))
            def _():
                marg[:B] = term

            @pl.when((x % 2 == 0) & (g != first))
            def _():
                marg[B:] = term[:H]

            @pl.when((x % 2 == 1) & (g == first))
            def _():
                marg[:H] = term[H:]

            @pl.when((x % 2 == 1) & (g != first))
            def _():
                marg[H:] = term

    return call(
        kernel,
        (n,),
        [
            whole((S, S)),
            whole((S, S)),
            pl.BlockSpec((S, B), lambda g, *_: (0, g)),
            pl.BlockSpec((B, B), lambda g, *_: (g, 0)),
        ],
        [pl.BlockSpec((B, B), lambda g, *_: (0, g)), whole((B + H, B))],
        [shape(B, n * B), shape(B + H, B)],
    )(ids, hi, lo, panel, diag)


def form_cov(hi, lo, uh, ul, th, tl, ph, pl_, jh, jl, place_slot, diag_of):
    for d in range(4):
        place_slot(d)

    @pl.loop(0, 4)
    def _(n):
        at = chunk(n)
        ph[:, at], pl_[:, at] = split(mm3(th[...], tl[...], hi[:, at], lo[:, at]))

    for n in range(4):
        at = slice(n * B, (n + 1) * B)
        above = n * B
        value = mm3(ph[: above + B], pl_[: above + B], uh[:, at], ul[:, at])
        jh[at, at], jl[at, at] = split(value[above:] + diag_of(n))
        if n:
            jh[:above, at], jl[:above, at] = split(value[:above])
            jh[at, :above], jl[at, :above] = split(value[:above].T)


def level_step(jh, jl, panel, diag, cross, marg):
    uh, ul = split(panel[...])
    value = -mm3(jh[...], jl[...], uh, ul)
    cross[...] = value
    xh, xl = split(value)
    th, tl = split(panel[...].T)
    for a in range(panel.shape[1] // B):
        at = slice(a * B, (a + 1) * B)
        both = mm(jnp.concatenate([th[at], tl[at]], 0), xh[:, at])
        marg[at] = diag[at] - (both[:B] + both[B:] + mm(th[at], xl[:, at]))


def level_specs(n, wide):
    cols = pl.BlockSpec((S, wide * B), lambda g, *_: (0, g))
    rows = pl.BlockSpec((wide * B, B), lambda g, *_: (g, 0))
    return [cols, rows], [cols, rows], [shape(S, n * B), shape(n * B, B)]


def mid_level(ids, hi, lo, part, part_core, d_own, d_core, panel, diag):
    n = panel.shape[1] // B

    def kernel(ids, hi, lo, own, core, d0, d1, panel, diag, cross, marg, jh, jl, uh, ul, th, tl, ph, pq):
        c = ids[0] % 2

        def place_slot(d):
            at = slice(d * B, (d + 1) * B)
            for ref, which in ((own, c), (core, 1 - c)):
                rows = pl.ds(pl.multiple_of(which * 512, 512), 512)
                v = ref[:, at]
                uh[rows, at], ul[rows, at] = split(v)
                th[at, rows], tl[at, rows] = split(v.T)

        def diag_of(s):
            rows = slice(s * PK, (s + 1) * PK)
            return unpack(d0[rows] + d1[rows])

        @pl.when(pl.program_id(0) == 0)
        def _():
            form_cov(hi, lo, uh, ul, th, tl, ph, pq, jh, jl, place_slot, diag_of)

        level_step(jh, jl, panel, diag, cross, marg)

    ins, outs, shapes = level_specs(n, 1)
    return call(
        kernel,
        (n,),
        [whole((S, S))] * 2
        + [whole(part.shape)] * 2
        + [whole((4 * PK, B))] * 2
        + ins,
        outs + [whole((S, S))] * 2,
        shapes + [shape(S, S, dtype=BF)] * 2,
        [pltpu.VMEM((S, S), BF)] * 6,
    )(ids, hi, lo, part, part_core, d_own, d_core, panel, diag)


def low_level(ids, hi, lo, parts, panel, diag):
    n = panel.shape[1] // B

    def kernel(ids, hi, lo, *refs):
        own_lo, own_hi, left_lo, right_hi, from_left, from_right = refs[:6]
        panel, diag, cross, marg = refs[6:10]
        uh, ul, th, tl, ph, pq, jh, jl, dd = refs[10:]
        x = ids[1]
        lows = (own_lo, from_right.at[:LO], from_left.at[HI:], left_lo)
        highs = (own_hi, right_hi, from_right.at[LO:], from_left.at[:HI])

        def place_slot(d):
            slot = (x + d) % 4
            at = chunk(slot)
            v = jnp.concatenate([lows[d][...], highs[d][: S - LO]], 0)
            uh[:, at], ul[:, at] = split(v)
            th[at, :], tl[at, :] = split(v.T)
            dd[slot] = highs[d][S - LO :]

        @pl.when(pl.program_id(0) == 0)
        def _():
            form_cov(hi, lo, uh, ul, th, tl, ph, pq, jh, jl, place_slot, lambda s: unpack(dd[s]))

        level_step(jh, jl, panel, diag, cross, marg)

    ins, outs, shapes = level_specs(n, 2)
    return call(
        kernel,
        (n // 2,),
        [whole((S, S))] * 2 + [whole(p.shape) for p in parts] + ins,
        outs,
        shapes,
        [pltpu.VMEM((S, S), BF)] * 8 + [pltpu.VMEM((4, PK, B), F32)],
    )(ids, hi, lo, *parts, panel, diag)


def local(
    sigma_top, panel_top, diag_top, panel_mid, diag_mid, pattern_mid, panel_low, diag_low, pattern_low
):
    leaf = lax.axis_index("leaf")
    x = lax.axis_index("rows")
    ids = jnp.stack([leaf, x]).astype(jnp.int32)
    side = leaf // 2 % 2
    half = S // 2

    panel_other, diag_other = partner((panel_mid, diag_mid), 0)
    quad = jnp.where(side == 0, sigma_top[:, :half], sigma_top[:, half:])
    quad_far = partner(quad, 1)
    to_far, keep_far, d_far = select_top(ids, pattern_mid, panel_top, diag_top, 1)
    core_far = partner(to_far, 0)

    plus, minus, one_lo, three_hi, own_lo, own_hi = select_low(
        ids, pattern_low, panel_mid, panel_other, diag_mid, diag_other
    )
    plus, minus, quad_far, sigma_ = tie(plus, minus, quad_far, sigma_top)
    r_plus = shift(plus, 1)
    r_minus = shift(minus, -1)
    sig_core = partner(sigma_, 0)
    quad_core = partner(quad_far, 0)

    far_sum, sig_core = tie(keep_far + core_far, sig_core)
    recv = partner(far_sum, 1)
    hi, lo = join_sigma(ids, sigma_top, sig_core, quad_far, quad_core)
    cross_top, marginal_top = top_level(ids, hi, lo, panel_top, diag_top)
    r_plus, r_minus, cross_top, panel_top_, d_far = tie(r_plus, r_minus, cross_top, panel_top, d_far)
    to_own, keep_own, d_keep = select_top(ids, pattern_mid, panel_top_, diag_top, 0)
    core_own = partner(to_own, 0)
    d_recv = partner(d_far, 1)
    r_one_lo = shift(one_lo + r_plus[:LO], 1)
    r_three_hi = shift(three_hi + r_minus[:HI], -1)
    own_lo = own_lo + r_minus[HI:]
    own_hi = own_hi + r_plus[LO:]

    own_lo = own_lo + r_one_lo
    own_hi = own_hi + r_three_hi
    own_lo, own_hi, keep_own = tie(own_lo, own_hi, keep_own)
    left_lo, right_hi = shift(own_lo, 1), shift(own_hi, -1)

    left_lo, right_hi, recv, d_recv = tie(left_lo, right_hi, recv, d_recv)
    part = keep_own + core_own + recv
    part_core = partner(part, 0)
    d_part = d_keep + d_recv
    d_core = partner(d_part, 0)

    next_plus = jnp.concatenate([own_hi, left_lo], 0)
    next_minus = jnp.concatenate([own_lo, right_hi], 0)
    next_plus, next_minus, hi = tie(next_plus, next_minus, hi)
    from_left = shift(next_plus, 1)
    from_right = shift(next_minus, -1)
    cross_mid, marginal_mid, mid_hi, mid_lo = mid_level(
        ids, hi, lo, part, part_core, d_part, d_core, panel_mid, diag_mid
    )
    cross_low, marginal_low = low_level(
        ids,
        mid_hi,
        mid_lo,
        [own_lo, own_hi, left_lo, right_hi, from_left, from_right],
        panel_low,
        diag_low,
    )
    return (cross_top, marginal_top, cross_mid, marginal_mid, cross_low, marginal_low)


def solution(mesh):
    return jax.shard_map(
        local,
        mesh=mesh,
        in_specs=(
            P("leaf", None),
            P(None, "leaf"),
            P("leaf", None),
            P(None, ("leaf", "rows")),
            P(("leaf", "rows"), None),
            P(),
            P(None, ("leaf", "rows")),
            P(("leaf", "rows"), None),
            P(),
        ),
        out_specs=(
            P("rows", "leaf"),
            P(("leaf", "rows"), None),
            P(None, ("leaf", "rows")),
            P(("leaf", "rows"), None),
            P(None, ("leaf", "rows")),
            P(("leaf", "rows"), None),
        ),
        check_vma=False,
    )
```

```python
import jax
import jax.numpy as jnp
from jax import lax
from jax.experimental import pallas as pl
from jax.experimental.pallas import tpu as pltpu
from jax.sharding import PartitionSpec as P

F32 = jnp.float32
BF = jnp.bfloat16
B = 256
H = 128
S = 1024
LO = 576
PK = 136
HI = S - LO + PK
VMEM = 56 * 2**20


def shift(value, step):
    n = lax.axis_size("rows")
    return lax.ppermute(value, "rows", [(i, (i + step) % n) for i in range(n)])


def partner(value, bit):
    n = lax.axis_size("leaf")
    return lax.ppermute(value, "leaf", [(i, i ^ (1 << bit)) for i in range(n)])


def tie(*values):
    return lax.optimization_barrier(values)


def split(v):
    hi = v.astype(BF)
    return hi, (v - hi.astype(F32)).astype(BF)


def mm(a, b):
    return lax.dot_general(a, b, (((1,), (0,)), ((), ())), preferred_element_type=F32)


def mm3(ah, al, bh, bl):
    return mm(ah, bh) + mm(ah, bl) + mm(al, bh)


def chunk(i):
    return pl.ds(pl.multiple_of(i * B, B), B)


def pack(d):
    a, b, c = d[:H, :H], d[:H, H:], d[H:, H:]
    row = lax.broadcasted_iota(jnp.int32, (H, H), 0)
    col = lax.broadcasted_iota(jnp.int32, (H, H), 1)
    fold = jnp.where(col >= row, a, c)
    diag = jnp.sum(jnp.where(col == row, c, 0.0), axis=0, keepdims=True)
    low = jnp.broadcast_to(diag, (PK - H, H))
    return jnp.concatenate(
        [jnp.concatenate([b, fold], 1), jnp.concatenate([low, jnp.zeros_like(low)], 1)], 0
    )


def unpack(p):
    b, fold, diag = p[:H, :H], p[:H, H:], p[H : H + 1, :H]
    row = lax.broadcasted_iota(jnp.int32, (H, H), 0)
    col = lax.broadcasted_iota(jnp.int32, (H, H), 1)
    turned = fold.T
    a = jnp.where(col >= row, fold, turned)
    c = jnp.where(col == row, diag, jnp.where(col < row, fold, turned))
    return jnp.concatenate([jnp.concatenate([a, b], 1), jnp.concatenate([b.T, c], 1)], 0)


def call(kernel, grid, in_specs, out_specs, out_shape, scratch=(), prefetch=1):
    return pl.pallas_call(
        kernel,
        grid_spec=pltpu.PrefetchScalarGridSpec(
            num_scalar_prefetch=prefetch,
            grid=grid,
            in_specs=in_specs,
            out_specs=out_specs,
            scratch_shapes=scratch,
        ),
        out_shape=out_shape,
        compiler_params=pltpu.CompilerParams(vmem_limit_bytes=VMEM),
        cost_estimate=pl.CostEstimate(flops=1024, bytes_accessed=1024, transcendentals=0),
    )


def whole(shape):
    return pl.BlockSpec(shape, lambda g, *_: (0,) * len(shape))


def shape(*dims, dtype=F32):
    return jax.ShapeDtypeStruct(dims, dtype)


def top_entry(ids, pattern, far, slot):
    child = ids[0] // 2
    return pattern[child + far * (1 - 2 * (child % 2)), slot]


def select_top(ids, pattern, panel, diag, far):
    n = panel.shape[1] // B
    half = S // 2

    def panel_spec(other):
        def index(g, ids, pattern):
            c = ids[0] % 2
            return (1 - c if other else c), top_entry(ids, pattern, far, g) % n

        return pl.BlockSpec((half, B), index)

    def kernel(ids, pattern, p0, p1, dia, to, keep, d):
        held = top_entry(ids, pattern, far, pl.program_id(0)) // n == ids[0] % 4
        to[...] = jnp.where(held, p0[...], 0.0)
        keep[...] = jnp.where(held, p1[...], 0.0)
        d[...] = jnp.where(held, pack(dia[...]), 0.0)

    wide = pl.BlockSpec((half, B), lambda g, *_: (0, g))
    tall = pl.BlockSpec((PK, B), lambda g, *_: (g, 0))
    rows = pl.BlockSpec((B, B), lambda g, ids, pattern: (top_entry(ids, pattern, far, g) % n, 0))
    return call(
        kernel,
        (4,),
        [panel_spec(True), panel_spec(False), rows],
        [wide, wide, tall],
        [shape(half, S), shape(half, S), shape(4 * PK, B)],
        prefetch=2,
    )(ids, pattern, panel, panel, diag)


def ring_step(g):
    return jnp.where(g == 0, 2, jnp.where(g == 1, 1, jnp.where(g == 2, 3, 0)))


def low_entry(ids, pattern, g):
    return pattern[ids[0], (ids[1] + ring_step(g)) % 4]


def select_low(ids, pattern, panel, panel_other, diag, diag_other):
    n = panel.shape[1] // B

    def kernel(ids, pattern, mine, other, d_mine, d_other, plus, minus, one_lo, three_hi, own_lo, own_hi):
        g = pl.program_id(0)
        b = low_entry(ids, pattern, g)
        spot = b // n
        here = spot % 4 == ids[1]
        own = spot // 4 == ids[0] % 2
        lows = (plus.at[:LO], one_lo, minus.at[HI:], own_lo)
        highs = (minus.at[:HI], plus.at[LO:], three_hi, own_hi)
        for t in range(4):

            @pl.when(g == t)
            def _(t=t):
                low, high = lows[t], highs[t]

                def chosen(u, v):
                    return jnp.where(here, jnp.where(own, u, v), 0.0)

                low[...] = chosen(mine[:LO], other[:LO])
                high[: S - LO] = chosen(mine[LO:], other[LO:])
                high[S - LO :] = pack(chosen(d_mine[...], d_other[...]))

    cols = pl.BlockSpec((S, B), lambda g, ids, pattern: (0, low_entry(ids, pattern, g) % n))
    rows = pl.BlockSpec((B, B), lambda g, ids, pattern: (low_entry(ids, pattern, g) % n, 0))
    outs = [(LO + HI, B), (LO + HI, B), (LO, B), (HI, B), (LO, B), (HI, B)]
    return call(
        kernel,
        (4,),
        [cols, cols, rows, rows],
        [whole(o) for o in outs],
        [shape(*o) for o in outs],
        prefetch=2,
    )(ids, pattern, panel, panel_other, diag, diag_other)


def join_sigma(ids, own, own_core, far, far_core):
    def kernel(ids, own, own_core, far, far_core, hi, lo):
        side, core = ids[0] // 2 % 2, ids[0] % 2
        near_half = pl.ds(pl.multiple_of(side * 512, 512), 512)
        far_half = pl.ds(pl.multiple_of((1 - side) * 512, 512), 512)
        for ref, quad, c in ((own, far, core), (own_core, far_core, 1 - core)):
            rows = chunk(2 * side + c)
            hi[rows, :], lo[rows, :] = split(ref[...])
            hi[far_half, rows], lo[far_half, rows] = split(ref[:, far_half].T)
            rows = chunk(2 * (1 - side) + c)
            hi[rows, far_half], lo[rows, far_half] = split(quad[...])

    return call(
        kernel,
        (1,),
        [whole((B, S)), whole((B, S)), whole((B, 512)), whole((B, 512))],
        [whole((S, S))] * 2,
        [shape(S, S, dtype=BF)] * 2,
    )(ids, own, own_core, far, far_core)


def top_level(ids, hi, lo, panel, diag):
    n = panel.shape[1] // B

    def kernel(ids, hi, lo, panel, diag, cross, marg):
        g = pl.program_id(0)
        x = ids[1]
        first = x // 2 * 3 + x % 2
        uh, ul = split(panel[...])
        mine = chunk(x)
        cross[...] = -mm3(hi[mine, :], lo[mine, :], uh, ul)

        @pl.when((g == first) | (g == first + 1))
        def _():
            yh, yl = split(mm3(hi[...], lo[...], uh, ul))
            th, tl = split(panel[...].T)
            term = diag[...] + mm3(th, tl, yh, yl)

            @pl.when((x % 2 == 0) & (g == first))
            def _():
                marg[:B] = term

            @pl.when((x % 2 == 0) & (g != first))
            def _():
                marg[B:] = term[:H]

            @pl.when((x % 2 == 1) & (g == first))
            def _():
                marg[:H] = term[H:]

            @pl.when((x % 2 == 1) & (g != first))
            def _():
                marg[H:] = term

    return call(
        kernel,
        (n,),
        [
            whole((S, S)),
            whole((S, S)),
            pl.BlockSpec((S, B), lambda g, *_: (0, g)),
            pl.BlockSpec((B, B), lambda g, *_: (g, 0)),
        ],
        [pl.BlockSpec((B, B), lambda g, *_: (0, g)), whole((B + H, B))],
        [shape(B, n * B), shape(B + H, B)],
    )(ids, hi, lo, panel, diag)


def form_cov(hi, lo, uh, ul, th, tl, ph, pl_, jh, jl, place_slot, diag_of):
    for d in range(4):
        place_slot(d)

    @pl.loop(0, 4)
    def _(n):
        at = chunk(n)
        ph[:, at], pl_[:, at] = split(mm3(th[...], tl[...], hi[:, at], lo[:, at]))

    for n in range(4):
        at = slice(n * B, (n + 1) * B)
        above = n * B
        value = mm3(ph[: above + B], pl_[: above + B], uh[:, at], ul[:, at])
        jh[at, at], jl[at, at] = split(value[above:] + diag_of(n))
        if n:
            jh[:above, at], jl[:above, at] = split(value[:above])
            jh[at, :above], jl[at, :above] = split(value[:above].T)


def level_step(jh, jl, panel, diag, cross, marg):
    uh, ul = split(panel[...])
    value = -mm3(jh[...], jl[...], uh, ul)
    cross[...] = value
    xh, xl = split(value)
    th, tl = split(panel[...].T)
    for a in range(panel.shape[1] // B):
        at = slice(a * B, (a + 1) * B)
        both = mm(jnp.concatenate([th[at], tl[at]], 0), xh[:, at])
        marg[at] = diag[at] - (both[:B] + both[B:] + mm(th[at], xl[:, at]))


def level_specs(n, wide):
    cols = pl.BlockSpec((S, wide * B), lambda g, *_: (0, g))
    rows = pl.BlockSpec((wide * B, B), lambda g, *_: (g, 0))
    return [cols, rows], [cols, rows], [shape(S, n * B), shape(n * B, B)]


def mid_level(ids, hi, lo, part, part_core, d_own, d_core, panel, diag):
    n = panel.shape[1] // B

    def kernel(ids, hi, lo, own, core, d0, d1, panel, diag, cross, marg, jh, jl, uh, ul, th, tl, ph, pq):
        c = ids[0] % 2

        def place_slot(d):
            at = slice(d * B, (d + 1) * B)
            for ref, which in ((own, c), (core, 1 - c)):
                rows = pl.ds(pl.multiple_of(which * 512, 512), 512)
                v = ref[:, at]
                uh[rows, at], ul[rows, at] = split(v)
                th[at, rows], tl[at, rows] = split(v.T)

        def diag_of(s):
            rows = slice(s * PK, (s + 1) * PK)
            return unpack(d0[rows] + d1[rows])

        @pl.when(pl.program_id(0) == 0)
        def _():
            form_cov(hi, lo, uh, ul, th, tl, ph, pq, jh, jl, place_slot, diag_of)

        level_step(jh, jl, panel, diag, cross, marg)

    ins, outs, shapes = level_specs(n, 1)
    return call(
        kernel,
        (n,),
        [whole((S, S))] * 2
        + [whole(part.shape)] * 2
        + [whole((4 * PK, B))] * 2
        + ins,
        outs + [whole((S, S))] * 2,
        shapes + [shape(S, S, dtype=BF)] * 2,
        [pltpu.VMEM((S, S), BF)] * 6,
    )(ids, hi, lo, part, part_core, d_own, d_core, panel, diag)


def low_level(ids, hi, lo, parts, panel, diag):
    n = panel.shape[1] // B

    def kernel(ids, hi, lo, *refs):
        own_lo, own_hi, left_lo, right_hi, from_left, from_right = refs[:6]
        panel, diag, cross, marg = refs[6:10]
        uh, ul, th, tl, ph, pq, jh, jl, dd = refs[10:]
        x = ids[1]
        lows = (own_lo, from_right.at[:LO], from_left.at[HI:], left_lo)
        highs = (own_hi, right_hi, from_right.at[LO:], from_left.at[:HI])

        def place_slot(d):
            slot = (x + d) % 4
            at = chunk(slot)
            v = jnp.concatenate([lows[d][...], highs[d][: S - LO]], 0)
            uh[:, at], ul[:, at] = split(v)
            th[at, :], tl[at, :] = split(v.T)
            dd[slot] = highs[d][S - LO :]

        @pl.when(pl.program_id(0) == 0)
        def _():
            form_cov(hi, lo, uh, ul, th, tl, ph, pq, jh, jl, place_slot, lambda s: unpack(dd[s]))

        level_step(jh, jl, panel, diag, cross, marg)

    ins, outs, shapes = level_specs(n, 2)
    return call(
        kernel,
        (n // 2,),
        [whole((S, S))] * 2 + [whole(p.shape) for p in parts] + ins,
        outs,
        shapes,
        [pltpu.VMEM((S, S), BF)] * 8 + [pltpu.VMEM((4, PK, B), F32)],
    )(ids, hi, lo, *parts, panel, diag)


def local(
    sigma_top, panel_top, diag_top, panel_mid, diag_mid, pattern_mid, panel_low, diag_low, pattern_low
):
    leaf = lax.axis_index("leaf")
    x = lax.axis_index("rows")
    ids = jnp.stack([leaf, x]).astype(jnp.int32)
    side = leaf // 2 % 2
    half = S // 2

    panel_other, diag_other = partner((panel_mid, diag_mid), 0)
    quad = jnp.where(side == 0, sigma_top[:, :half], sigma_top[:, half:])
    quad_far = partner(quad, 1)
    to_far, keep_far, d_far = select_top(ids, pattern_mid, panel_top, diag_top, 1)
    core_far = partner(to_far, 0)

    to_own, keep_own, d_keep = select_top(ids, pattern_mid, panel_top, diag_top, 0)
    panel_other, to_own = tie(panel_other, to_own)

    plus, minus, one_lo, three_hi, own_lo, own_hi = select_low(
        ids, pattern_low, panel_mid, panel_other, diag_mid, diag_other
    )
    plus, minus, quad_far, sigma_ = tie(plus, minus, quad_far, sigma_top)
    r_plus = shift(plus, 1)
    r_minus = shift(minus, -1)
    sig_core = partner(sigma_, 0)
    quad_core = partner(quad_far, 0)

    far_sum, sig_core = tie(keep_far + core_far, sig_core)
    recv = partner(far_sum, 1)
    hi, lo = join_sigma(ids, sigma_top, sig_core, quad_far, quad_core)
    cross_top, marginal_top = top_level(ids, hi, lo, panel_top, diag_top)
    r_plus, r_minus, cross_top, to_own, d_far = tie(r_plus, r_minus, cross_top, to_own, d_far)
    core_own = partner(to_own, 0)
    d_recv = partner(d_far, 1)
    r_one_lo = shift(one_lo + r_plus[:LO], 1)
    r_three_hi = shift(three_hi + r_minus[:HI], -1)
    own_lo = own_lo + r_minus[HI:]
    own_hi = own_hi + r_plus[LO:]

    own_lo = own_lo + r_one_lo
    own_hi = own_hi + r_three_hi
    own_lo, own_hi, keep_own = tie(own_lo, own_hi, keep_own)
    left_lo, right_hi = shift(own_lo, 1), shift(own_hi, -1)

    left_lo, right_hi, recv, d_recv = tie(left_lo, right_hi, recv, d_recv)
    part = keep_own + core_own + recv
    part_core = partner(part, 0)
    d_part = d_keep + d_recv
    d_core = partner(d_part, 0)

    next_plus = jnp.concatenate([own_hi, left_lo], 0)
    next_minus = jnp.concatenate([own_lo, right_hi], 0)
    next_plus, next_minus, hi = tie(next_plus, next_minus, hi)
    from_left = shift(next_plus, 1)
    from_right = shift(next_minus, -1)
    cross_mid, marginal_mid, mid_hi, mid_lo = mid_level(
        ids, hi, lo, part, part_core, d_part, d_core, panel_mid, diag_mid
    )
    cross_low, marginal_low = low_level(
        ids,
        mid_hi,
        mid_lo,
        [own_lo, own_hi, left_lo, right_hi, from_left, from_right],
        panel_low,
        diag_low,
    )
    return (cross_top, marginal_top, cross_mid, marginal_mid, cross_low, marginal_low)


def solution(mesh):
    return jax.shard_map(
        local,
        mesh=mesh,
        in_specs=(
            P("leaf", None),
            P(None, "leaf"),
            P("leaf", None),
            P(None, ("leaf", "rows")),
            P(("leaf", "rows"), None),
            P(),
            P(None, ("leaf", "rows")),
            P(("leaf", "rows"), None),
            P(),
        ),
        out_specs=(
            P("rows", "leaf"),
            P(("leaf", "rows"), None),
            P(None, ("leaf", "rows")),
            P(("leaf", "rows"), None),
            P(None, ("leaf", "rows")),
            P(("leaf", "rows"), None),
        ),
        check_vma=False,
    )
```
